128 devices in a mesh: rep: 16 (over x_lo, y, core), tp: 8 (over x_hi, z).
Axes of the slice: x: 4 (x_hi: 2, x_lo: 2; x = x_hi * 2 + x_lo), y: 4, z: 4, core: 2. Of those that a mesh axis runs over, the one named last changes fastest.
Arguments:
- tokens: bfloat16 [16, 4096, 5120], P('rep', 'tp'), may hold values from -6 to 6
- cotangent: bfloat16 [16, 4096, 1024], P('rep', 'tp'), may hold values from -6 to 6
- params: float32 [16, 5120, 1024], P('rep', 'tp'), may hold values from -0.078125 to 0.078125
- tracker: float32 [16, 5120, 1024], P('rep', 'tp'), may hold values from -6 to 6
- grad_old: float32 [16, 5120, 1024], P('rep', 'tp'), may hold values from -6 to 6
- step: int32 [1], replicated, may hold values from 0 to 2
Outputs:
- keys: bfloat16 [16, 4096, 1024], P('rep', 'tp')
- input_grad: bfloat16 [16, 4096, 5120], P('rep', 'tp')
- new_params: float32 [16, 5120, 1024], P('rep', 'tp')
- new_tracker: float32 [16, 5120, 1024], P('rep', 'tp')
The draws below stay inside these ranges and needn't reach their ends.
All inputs are finite; a program needn't handle non-finite values.
Results may differ from the reference program's by a relative error of at most 0.009.
Values may be sent and summed in bfloat16 or wider, within the bound.
A program may use at most 128 MiB of HBM per device.

```python
import jax
import jax.numpy as jnp
from jax import lax

D = 5120
KV = 1024
TOK_DEV = 512
TOKENS = 4096
REPS = 16
N_TP = 8


def steps_of(stream_key, extent, shards, low, largest):
    def one(dim, blocks):
        draws = jax.random.uniform(jax.random.fold_in(jax.random.fold_in(stream_key, 6), dim), (blocks,), jnp.float32, low / len(shards), largest / len(shards))
        return jnp.repeat(jnp.exp(draws), extent[dim] // blocks).reshape((-1,) + (1,) * (len(extent) - dim - 1))

    factor_of = one(*shards[0])
    for cut in shards[1:]:
        factor_of = factor_of * one(*cut)
    return factor_of


def centred(key, shape, width, bound, shards=(), held_as=jnp.bfloat16):
    values = width * jax.random.normal(key, shape, jnp.float32)
    if shards:
        values = values * steps_of(key, shape, shards, -0.22, 0.18)
    return jnp.clip(values, -bound, bound).astype(held_as)


def setup_inputs(seed: int = 0) -> dict:
    streams_of = jax.random.split(jax.random.key(seed), 7)
    tokens = centred(streams_of[0], (REPS, TOKENS, D), 1.0, 6.0, ((0, 16), (1, 8)))
    cotangent = centred(streams_of[1], (REPS, TOKENS, KV), 1.0, 6.0, ((0, 16), (1, 8)))
    params = centred(streams_of[2], (REPS, D, KV), D ** -0.5, 0.078125, ((0, 16), (1, 8)), jnp.float32)
    tracker = centred(streams_of[3], (REPS, D, KV), 1.0, 6.0, ((0, 16), (1, 8)), jnp.float32)
    grad_old = centred(streams_of[4], (REPS, D, KV), 1.0, 6.0, ((0, 16), (1, 8)), jnp.float32)
    step = jax.random.randint(streams_of[5], (1,), 0, 3).astype(jnp.int32)
    return {"tokens": tokens, "cotangent": cotangent, "params": params, "tracker": tracker, "grad_old": grad_old, "step": step}


def one_replica(items):
    tok_rows, cot_rows, param_rows = items
    weights = param_rows.astype(jnp.bfloat16)
    keys = jnp.dot(tok_rows, weights, preferred_element_type=jnp.float32).astype(jnp.bfloat16)
    back = lax.dot_general(cot_rows, weights, (((1,), (1,)), ((), ())), preferred_element_type=jnp.float32).astype(jnp.bfloat16)
    scale = 1.0 / jnp.sqrt(jnp.float32(TOKENS))
    tok_blocks = tok_rows.reshape(N_TP, TOK_DEV, D)
    cot_blocks = cot_rows.reshape(N_TP, TOK_DEV, KV)

    def add_block(total, pair):
        term = lax.dot_general(pair[0], pair[1], (((0,), (0,)), ((), ())), preferred_element_type=jnp.float32) * scale
        return (total + term.astype(jnp.bfloat16).astype(jnp.float32), None)
    grad, unused = lax.scan(add_block, jnp.zeros((D, KV), jnp.float32), (tok_blocks, cot_blocks))
    return (keys, back, grad)

def reference(tokens, cotangent, params, tracker, grad_old, step):
    keys, back, grad = lax.map(one_replica, (tokens, cotangent, params))
    half = params - 0.01 * tracker
    shift_bits = jnp.left_shift(jnp.int32(1), step[0].astype(jnp.int32))
    partners = jnp.bitwise_xor(jnp.arange(REPS, dtype=jnp.int32), shift_bits)
    new_params = 0.5 * (half + jnp.take(half, partners, axis=0))
    new_tracker = 0.5 * (tracker + jnp.take(tracker, partners, axis=0)) + grad - grad_old
    return (keys, back, new_params, new_tracker)
```

```python
import functools

import jax
import jax.numpy as jnp
from jax import lax
from jax.experimental import pallas as pl
from jax.experimental.pallas import tpu as pltpu
from jax.sharding import PartitionSpec as P

MESH = pl.DeviceIdType.MESH
Q = 4
NZ = 4
DEPTH = 3
F32, BF16 = jnp.float32, jnp.bfloat16
NT = (((1,), (1,)), ((), ()))
TN = (((0,), (0,)), ((), ()))


def kernel(
    level, scale,
    tok_h, cot_h, par_h, trk_h, old_h,
    keys_h, back_h, npar_h, ntrk_h,
    tok, cot, par, trk, old, w, part, rx, zh, zf, rt, mine, far, acc, kout, bout,
    load, store, bstore, xs, xr, ps, pr, ms, mr, fs, fr,
):
    rep, tp = lax.axis_index("rep"), lax.axis_index("tp")
    line, z = lax.div(tp, NZ), lax.rem(tp, NZ)
    rows = par.shape[0]
    wide = par.shape[1] // Q
    stride = 2**level
    bit = lax.rem(lax.div(rep, stride), 2)
    twin = (rep, lax.rem(tp + NZ, 2 * NZ))
    above = (rep, line * NZ + lax.rem(z + 1, NZ))
    below = (rep, line * NZ + lax.rem(z + NZ - 1, NZ))
    partner = (rep + stride * (1 - 2 * bit), tp)

    def col(q):
        return pl.ds(q * wide, wide)

    loads = [
        pltpu.make_async_copy(par_h.at[0, :, col(q)], par.at[:, col(q)], load.at[q]) for q in range(Q)
    ]
    loads.append(pltpu.make_async_copy(trk_h.at[0], trk, load.at[Q]))
    loads.append(pltpu.make_async_copy(cot_h.at[0], cot, load.at[Q + 1]))
    loads.append(pltpu.make_async_copy(tok_h.at[0], tok, load.at[Q + 2]))
    loads.append(pltpu.make_async_copy(old_h.at[0], old, load.at[Q + 3]))
    for c in loads:
        c.start()

    barrier = pltpu.get_barrier_semaphore()
    for other in (twin, above, below, partner):
        pl.semaphore_signal(barrier, 1, device_id=other, device_id_type=MESH)

    lo, hi = pl.ds(0, rows // 2), pl.ds(rows // 2, rows // 2)
    xl = [(("w", 4, q), w.at[0, q], w.at[4, q]) for q in range(Q)]
    order = [(2, 0), (2, 1), (2, 2), (1, 2), (3, 0), (1, 3), (3, 1), (1, 0), (3, 2), (1, 1), (3, 3)]
    order += [(0, q) for q in range(Q)]
    xl += [(("rx", j, q), part.at[4 + j, q], rx.at[j, q]) for j, q in order]
    pl_ = [(("w", 1, q), w.at[0, q], w.at[1, q]) for q in (0, 1, 2, 3)]
    pl_ += [(("rt", 0, 0), part.at[6, 3, lo], rt.at[0])]
    pl_ += [(("w", 2, q), w.at[1, q], w.at[2, q]) for q in (0, 1)]
    pl_ += [(("w", 5, q), w.at[4, q], w.at[5, q]) for q in (0, 1, 2, 3)]
    pl_ += [(("w", 6, q), w.at[5, q], w.at[6, q]) for q in (0, 1)]
    pl_ += [(("zh", 0, q), part.at[2, q], zh.at[0, q]) for q in (0, 1)]
    pl_ += [(("zf", 0, q), part.at[1, q], zf.at[0, q]) for q in (2, 3, 0, 1)]
    ml = [(("w", 3, q), w.at[0, q], w.at[3, q]) for q in (2, 3, 0, 1)]
    ml += [(("rt", 1, 0), part.at[6, 3, hi], rt.at[1])]
    ml += [(("w", 2, q), w.at[3, q], w.at[2, q]) for q in (2, 3)]
    ml += [(("w", 7, q), w.at[4, q], w.at[7, q]) for q in (2, 3, 0, 1)]
    ml += [(("w", 6, q), w.at[7, q], w.at[6, q]) for q in (2, 3)]
    ml += [(("zh", 1, q), part.at[2, q], zh.at[1, q - 2]) for q in (2, 3)]
    ml += [(("zf", 1, q), part.at[3, q], zf.at[1, q]) for q in (0, 1, 2, 3)]
    links = {}
    arrives = {}
    for name, items, dev, ssem, rsem in (
        ("x", xl, twin, xs, xr), ("p", pl_, above, ps, pr), ("m", ml, below, ms, mr),
    ):
        links[name] = []
        for i, (tag, src, dst) in enumerate(items):
            c = pltpu.make_async_remote_copy(
                src, dst, ssem.at[i], rsem.at[i], device_id=dev, device_id_type=MESH
            )
            links[name].append((tag, c))
            arrives[tag] = c
    pair = [
        pltpu.make_async_remote_copy(
            mine.at[i], far.at[i], fs.at[i], fr.at[i], device_id=partner, device_id_type=MESH
        )
        for i in range(2)
    ]
    seen = set()
    sent = {"x": 0, "p": 0, "m": 0}

    def need(*tag):
        if tag not in seen:
            seen.add(tag)
            arrives[tag].wait_recv()

    def widen(x):
        return x.astype(F32)

    def add_to(dst, *srcs):
        @pl.loop(0, dst.shape[0] // 80)
        def _(i):
            r = pl.ds(pl.multiple_of(i * 80, 80), 80)
            total = widen(dst[r, :])
            for s in srcs:
                total = total + widen(s[r, :])
            dst[r, :] = total.astype(BF16)

    def prepare(link, tag):
        kind, j, q = tag
        if kind == "w" and j in (5, 7):
            need("w", 4, q)
        if kind == "w" and j == 6:
            need("w", 5 if link == "p" else 7, q)
        if kind == "w" and j == 2:
            need("w", 1 if link == "p" else 3, q)
        if kind == "rx" and q == 3 and j in (1, 3):
            i = 0 if j == 1 else 1
            need("rt", i, 0)
            add_to(part.at[4 + j, 3, lo if i == 0 else hi], rt.at[i])
        if kind == "zh" and q != 3:
            need("rx", 2, q)
            add_to(part.at[2, q], rx.at[2, q])
        if kind == "zf":
            mid = 1 if link == "p" else 3
            need("rx", mid, q)
            more = [rx.at[mid, q]]
            if link == "p" and q in (0, 1):
                need("zh", 0, q)
                more.append(zh.at[0, q])
            if link == "m" and q in (2, 3):
                need("zh", 1, q)
                more.append(zh.at[1, q - 2])
            add_to(part.at[mid, q], *more)

    def issue(link, upto):
        while sent[link] < min(upto, len(links[link])):
            i = sent[link]
            tag, c = links[link][i]
            if i >= DEPTH:
                links[link][i - DEPTH][1].wait_send()
            prepare(link, tag)
            c.start()
            sent[link] = i + 1

    def cols_of(j):
        owner = lax.rem(line + lax.div(j, NZ), 2) * NZ + lax.rem(z + lax.rem(j, NZ), NZ)
        return pl.ds(pl.multiple_of(owner * rows, 128), rows)

    def partials(j):
        c = cols_of(j)

        @pl.loop(0, Q)
        def _(q):
            qc = pl.ds(pl.multiple_of(q * wide, 128), wide)
            g = lax.dot_general(tok[:, c], cot[:, qc], TN, preferred_element_type=F32)
            part[j, q] = (g * scale).astype(BF16)

    flight = [None, None]
    stores = []

    def use(slot):
        if slot:
            for q in range(Q):
                need("w", slot, q)
        j = (0, 3, 2, 1)[slot % 4] + 4 * (slot // 4)
        c = cols_of(j)
        b = len(stores) % 2
        if flight[b] is not None:
            flight[b].wait()

        @pl.loop(0, Q)
        def _(q):
            qc = pl.ds(pl.multiple_of(q * wide, 128), wide)
            t = jnp.dot(tok[:, c], w[slot, q], preferred_element_type=F32)
            if slot == 0:
                acc[:, qc] = t
            else:
                acc[:, qc] += t

        half = tok.shape[0] // 2

        @pl.loop(0, 2)
        def _(m):
            r = pl.ds(pl.multiple_of(m * half, half), half)
            t = lax.dot_general(cot[r, col(0)], w[slot, 0], NT, preferred_element_type=F32)
            for q in range(1, Q):
                t = t + lax.dot_general(cot[r, col(q)], w[slot, q], NT, preferred_element_type=F32)
            bout[b, r, :] = t.astype(BF16)

        flight[b] = pltpu.make_async_copy(bout.at[b], back_h.at[0, :, c], bstore.at[b])
        flight[b].start()
        stores.append(slot)

    for q in range(Q):
        loads[q].wait()
        w[0, q] = par[:, col(q)].astype(BF16)
        if q == 0:
            pl.semaphore_wait(barrier, 4)
            issue("x", 1)
            issue("p", 1)
    issue("m", 1)
    for n in range(2, DEPTH + 1):
        for link in ("x", "p", "m"):
            issue(link, n)

    loads[Q].wait()

    @pl.loop(0, rows // 32)
    def _(i):
        r = pl.ds(pl.multiple_of(i * 32, 32), 32)
        t = trk[r, :]
        mine[0, r, :] = (par[r, :] - 0.01 * t).astype(BF16)
        mine[1, r, :] = t.astype(BF16)

    pair[0].start()
    pair[1].start()
    loads[Q + 1].wait()
    loads[Q + 2].wait()
    loads[Q + 3].wait()

    @pl.loop(0, 8)
    def _(i):
        j = lax.rem(i + 6, 8)
        partials(j)

    def params_out():
        pair[0].wait_recv()

        @pl.loop(0, rows // 32)
        def _(i):
            r = pl.ds(pl.multiple_of(i * 32, 32), 32)
            half = par[r, :] - 0.01 * trk[r, :]
            par[r, :] = 0.5 * (half + widen(far[0, r, :]))

        c = pltpu.make_async_copy(par, npar_h.at[0], store.at[0])
        c.start()
        tail.append(c)

    def tracker_base():
        pair[1].wait_recv()

        @pl.loop(0, rows // 32)
        def _(i):
            r = pl.ds(pl.multiple_of(i * 32, 32), 32)
            trk[r, :] = 0.5 * (trk[r, :] + widen(far[1, r, :])) - old[r, :]

    def keys_out():
        @pl.loop(0, 8)
        def _(i):
            n = tok.shape[0] // 8
            r = pl.ds(pl.multiple_of(i * n, n), n)
            kout[r, :] = acc[r, :].astype(BF16)

        c = pltpu.make_async_copy(kout, keys_h.at[0], store.at[1])
        c.start()
        tail.append(c)

    tail = []
    work = {
        3: [lambda: use(0)],
        5: [lambda: use(1)],
        6: [lambda: use(3)],
        7: [lambda: use(4)],
        9: [lambda: use(2)],
        10: [params_out],
        11: [tracker_base],
        12: [lambda: use(5)],
        13: [lambda: use(7)],
        15: [lambda: use(6)],
        16: [keys_out],
    }
    longest = max(len(v) for v in links.values())
    for t in range(3, longest):
        for link in ("x", "p", "m"):
            issue(link, t + 1)
        for job in work.get(t, ()):
            job()

    for q in range(Q):
        need("zf", 0, q)
        need("zf", 1, q)
        need("rx", 0, q)

        @pl.loop(0, rows // 80)
        def _(i):
            r = pl.ds(pl.multiple_of(i * 80, 80), 80)
            g = widen(part[0, q, r, :]) + widen(rx[0, q, r, :])
            g = g + widen(zf[0, q, r, :]) + widen(zf[1, q, r, :])
            trk[r, col(q)] += g

        c = pltpu.make_async_copy(trk.at[:, col(q)], ntrk_h.at[0, :, col(q)], store.at[2 + q])
        c.start()
        tail.append(c)

    for name, items in links.items():
        for tag, c in items:
            if tag not in seen:
                seen.add(tag)
                c.wait_recv()
        for tag, c in items[max(0, len(items) - DEPTH):]:
            c.wait_send()
    for c in pair:
        c.wait_send()
    for c in flight + tail:
        c.wait()


def call(level, tokens, cotangent, params, tracker, grad_old):
    _, toks, d = tokens.shape
    _, rows, kv = params.shape
    wide = kv // Q
    scale = 1.0 / float(toks * 2 * NZ) ** 0.5
    sem = pltpu.SemaphoreType.DMA
    any_ = pl.BlockSpec(memory_space=pl.ANY)
    return pl.pallas_call(
        functools.partial(kernel, level, scale),
        out_shape=(
            jax.ShapeDtypeStruct(cotangent.shape, BF16),
            jax.ShapeDtypeStruct(tokens.shape, BF16),
            jax.ShapeDtypeStruct(params.shape, F32),
            jax.ShapeDtypeStruct(params.shape, F32),
        ),
        in_specs=[any_] * 5,
        out_specs=(any_,) * 4,
        scratch_shapes=[
            pltpu.VMEM((toks, d), BF16),
            pltpu.VMEM((toks, kv), BF16),
            pltpu.VMEM((rows, kv), F32),
            pltpu.VMEM((rows, kv), F32),
            pltpu.VMEM((rows, kv), F32),
            pltpu.VMEM((8, Q, rows, wide), BF16),
            pltpu.VMEM((8, Q, rows, wide), BF16),
            pltpu.VMEM((NZ, Q, rows, wide), BF16),
            pltpu.VMEM((2, 2, rows, wide), BF16),
            pltpu.VMEM((2, Q, rows, wide), BF16),
            pltpu.VMEM((2, rows // 2, wide), BF16),
            pltpu.VMEM((2, rows, kv), BF16),
            pltpu.VMEM((2, rows, kv), BF16),
            pltpu.VMEM((toks, kv), F32),
            pltpu.VMEM((toks, kv), BF16),
            pltpu.VMEM((2, toks, rows), BF16),
            sem((Q + 4,)), sem((Q + 2,)), sem((2,)),
            sem((19,)), sem((19,)), sem((19,)), sem((19,)), sem((19,)), sem((19,)), sem((2,)), sem((2,)),
        ],
        compiler_params=pltpu.CompilerParams(
            collective_id=level, has_side_effects=True, vmem_limit_bytes=60 << 20
        ),
        cost_estimate=pl.CostEstimate(
            flops=6 * toks * d * kv, bytes_accessed=26 << 20, transcendentals=0
        ),
        name=f"train_step_{level}",
    )(tokens, cotangent, params, tracker, grad_old)


def on_device(tokens, cotangent, params, tracker, grad_old, step):
    branches = [functools.partial(call, level) for level in range(3)]
    return lax.switch(
        jnp.clip(step[0], 0, 2), branches, tokens, cotangent, params, tracker, grad_old
    )


def solution(mesh):
    rows = P("rep", "tp", None)
    return jax.shard_map(
        on_device,
        mesh=mesh,
        in_specs=(rows,) * 5 + (P(),),
        out_specs=(rows,) * 4,
        check_vma=False,
    )
```

```python
import functools

import jax
import jax.numpy as jnp
from jax import lax
from jax.experimental import pallas as pl
from jax.experimental.pallas import tpu as pltpu
from jax.sharding import PartitionSpec as P

MESH = pl.DeviceIdType.MESH
Q = 4
NZ = 4
DEPTH = 2
F32, BF16 = jnp.float32, jnp.bfloat16
NT = (((1,), (1,)), ((), ()))
TN = (((0,), (0,)), ((), ()))


def kernel(
    level, scale,
    tok_h, cot_h, par_h, trk_h, old_h,
    keys, back, par, trk,
    tok, cot, old, w, part, tokb, cotb, zh, zf, mine, far, acc,
    load, xs, xr, ps, pr, ms, mr, fs, fr,
):
    rep, tp = lax.axis_index("rep"), lax.axis_index("tp")
    line, z = lax.div(tp, NZ), lax.rem(tp, NZ)
    toks = tok.shape[0]
    rows, kv = par.shape
    wide = kv // Q
    stride = 2**level
    bit = lax.rem(lax.div(rep, stride), 2)
    twin = (rep, lax.rem(tp + NZ, 2 * NZ))
    above = (rep, line * NZ + lax.rem(z + 1, NZ))
    below = (rep, line * NZ + lax.rem(z + NZ - 1, NZ))
    partner = (rep + stride * (1 - 2 * bit), tp)
    cut = rows * 2 // 5 // 128 * 128
    spans = ((0, cut), (cut, rows - cut))

    def col(q):
        return pl.ds(q * wide, wide)

    def cols_of(j, at=0, n=None, other=0):
        owner = lax.rem(line + other, 2) * NZ + lax.rem(z + j, NZ)
        return pl.ds(pl.multiple_of(owner * rows + at, 128), rows if n is None else n)

    loads = {"cot": pltpu.make_async_copy(cot_h.at[0], cot, load.at[0])}
    for q in range(Q):
        loads[q] = pltpu.make_async_copy(par_h.at[0, :, col(q)], par.at[:, col(q)], load.at[1 + q])
    loads["tok"] = pltpu.make_async_copy(tok_h.at[0], tok, load.at[Q + 1])
    loads["trk"] = pltpu.make_async_copy(trk_h.at[0], trk, load.at[Q + 2])
    loads["old"] = pltpu.make_async_copy(old_h.at[0], old, load.at[Q + 3])
    for c in loads.values():
        c.start()

    barrier = pltpu.get_barrier_semaphore()
    for other in (twin, above, below, partner):
        pl.semaphore_signal(barrier, 1, device_id=other, device_id_type=MESH)

    def shard(slot, q, src):
        return (("w", slot, q), 1.0, w.at[src, q], w.at[slot, q])

    def factor(j, i):
        at, n = spans[i]
        src = tok.at[:, cols_of(j, at, n, other=1)]
        return (("t", j, i), 2.0 * n / rows, src, tokb.at[j, :, pl.ds(at, n)])

    def finished(j, i):
        n = rows // 5
        r = pl.ds(i * n, n)
        k = 0 if j == 1 else 1
        return (("zf", k, i), 0.8, part.at[j - 1, r], zf.at[k, r])

    def passed(k, i):
        n = rows // 4
        return (
            ("zh", k, i), 1.0, part.at[1, pl.ds((2 * k + i) * n, n)], zh.at[k, pl.ds(i * n, n)],
        )

    half = toks // 2
    xl = [(("c", 0, i), 1.6, cot.at[pl.ds(i * half, half)], cotb.at[pl.ds(i * half, half)]) for i in (0, 1)]
    xl += [factor(2, 0), factor(2, 1)]
    xl += [shard(4, q, 0) for q in (0, 3, 1, 2)]
    xl += [factor(1, 0), factor(3, 0), factor(1, 1), factor(3, 1)]
    xl += [shard(6, q, 2) for q in (1, 2)]
    xl += [factor(0, 0), factor(0, 1)]
    up = [shard(1, q, 0) for q in (0, 1, 2, 3)]
    up += [shard(2, q, 1) for q in (0, 1)]
    up += [passed(0, 0), passed(0, 1)]
    up += [shard(5, q, 4) for q in (0, 3, 1, 2)]
    up += [shard(6, 0, 5)]
    up += [finished(1, i) for i in range(5)]
    down = [shard(3, q, 0) for q in (2, 3, 0, 1)]
    down += [shard(2, q, 3) for q in (2, 3)]
    down += [passed(1, 0), passed(1, 1)]
    down += [shard(7, q, 4) for q in (3, 0, 1, 2)]
    down += [shard(6, 3, 7)]
    down += [finished(3, i) for i in range(5)]
    made = {("p", "zh", False): 5.3, ("m", "zh", False): 5.3}
    made |= {("p", "zf", False): 10.2, ("m", "zf", False): 11.0}
    made |= {("p", "zf", True): 12.2, ("m", "zf", True): 13.4}
    links, arrives, program = {}, {}, []
    for name, items, dev, ssem, rsem in (
        ("x", xl, twin, xs, xr), ("p", up, above, ps, pr), ("m", down, below, ms, mr),
    ):
        links[name] = []
        ends = []
        for i, (tag, ticks, src, dst) in enumerate(items):
            c = pltpu.make_async_remote_copy(
                src, dst, ssem.at[i], rsem.at[i], device_id=dev, device_id_type=MESH
            )
            links[name].append((tag, c))
            arrives[tag] = c
            free = ends[i - DEPTH] if i >= DEPTH else 0.0
            program.append((max(free, made.get((name, tag[0], tag[2] > 1), 0.0)), name, i))
            ends.append((ends[-1] if ends else 0.0) + ticks)
    pair = [
        pltpu.make_async_remote_copy(
            mine.at[i], far.at[i], fs.at[i], fr.at[i], device_id=partner, device_id_type=MESH
        )
        for i in range(2)
    ]
    seen, ready = set(), set()

    def need(*tag):
        if tag not in seen:
            seen.add(tag)
            arrives[tag].wait_recv()

    def widen(x):
        return x.astype(F32)

    def add_rows(k, at, n):
        @pl.loop(0, n // 64)
        def _(i):
            r = pl.ds(pl.multiple_of(at + i * 64, 64), 64)
            s = pl.ds(pl.multiple_of(at + i * 64 - k * (rows // 2), 64), 64)
            part[2 * k, r, :] = (widen(part[2 * k, r, :]) + widen(zh[k, s, :])).astype(BF16)

    def prepare(link, tag):
        kind, j, q = tag
        if kind == "w" and j in (5, 7):
            need("w", 4, q)
        if kind == "w" and j == 6:
            need("w", {"x": 2, "p": 5, "m": 7}[link], q)
        if kind == "w" and j == 2:
            need("w", 1 if link == "p" else 3, q)
        if kind == "zh":
            assert {(2, 0), (2, 1)} <= ready
        if kind == "zf":
            assert (1 if link == "p" else 3, 0 if q < 2 else 1) in ready

    def issue(link, i):
        tag, c = links[link][i]
        if i >= DEPTH:
            links[link][i - DEPTH][1].wait_send()
        prepare(link, tag)
        c.start()

    def product(j, i, q, own=True, twins=True):
        at, n = spans[i]
        qc = pl.ds(pl.multiple_of(q * wide, 128), wide)
        g = 0.0
        if own:
            g = g + lax.dot_general(tok[:, cols_of(j, at, n)], cot[:, qc], TN, preferred_element_type=F32)
        if twins:
            g = g + lax.dot_general(
                tokb[j, :, pl.ds(at, n)], cotb[:, qc], TN, preferred_element_type=F32
            )
        return g * scale, pl.ds(at, n), qc

    def sums(j, i):
        need("c", 0, 0)
        need("c", 0, 1)
        need("t", j, i)

        @pl.loop(0, Q)
        def _(q):
            g, r, qc = product(j, i, q)
            part[j - 1, r, qc] = g.astype(BF16)

        if j != 2:
            k = 0 if j == 1 else 1
            need("zh", k, 0)
            need("zh", k, 1)
            at, n = spans[i]
            first, last = max(at, k * (rows // 2)), min(at + n, (k + 1) * (rows // 2))
            if last > first:
                add_rows(k, first, last - first)
        ready.add((j, i))

    def own_sum(i, own, twins):
        assert "base" in ready
        if twins:
            need("t", 0, i)

        @pl.loop(0, Q)
        def _(q):
            g, r, qc = product(0, i, q, own, twins)
            trk[r, qc] += g

    def add_finished(i):
        assert "base" in ready
        need("zf", 0, i)
        need("zf", 1, i)
        n = rows // 5

        @pl.loop(0, n // 32)
        def _(m):
            r = pl.ds(pl.multiple_of(i * n + m * 32, 32), 32)
            trk[r, :] += widen(zf[0, r, :]) + widen(zf[1, r, :])

    def use(slot):
        if slot:
            for q in range(Q):
                need("w", slot, q)
        c = cols_of((0, 3, 2, 1)[slot % 4], other=slot // 4)

        @pl.loop(0, Q)
        def _(q):
            qc = pl.ds(pl.multiple_of(q * wide, 128), wide)
            t = jnp.dot(tok[:, c], w[slot, q], preferred_element_type=F32)
            if slot == 0:
                acc[:, qc] = t
            else:
                acc[:, qc] += t

        @pl.loop(0, 2)
        def _(m):
            r = pl.ds(pl.multiple_of(m * half, half), half)
            t = lax.dot_general(cot[r, col(0)], w[slot, 0], NT, preferred_element_type=F32)
            for q in range(1, Q):
                t = t + lax.dot_general(cot[r, col(q)], w[slot, q], NT, preferred_element_type=F32)
            back[r, c] = t.astype(BF16)

    def send_pair():
        loads["trk"].wait()

        @pl.loop(0, rows // 32)
        def _(i):
            r = pl.ds(pl.multiple_of(i * 32, 32), 32)
            t = trk[r, :]
            mine[0, r, :] = (par[r, :] - 0.01 * t).astype(BF16)
            mine[1, r, :] = t.astype(BF16)

        pair[0].start()
        pair[1].start()

    def average():
        loads["old"].wait()
        pair[0].wait_recv()
        pair[1].wait_recv()

        @pl.loop(0, rows // 32)
        def _(i):
            r = pl.ds(pl.multiple_of(i * 32, 32), 32)
            t = trk[r, :]
            par[r, :] = 0.5 * ((par[r, :] - 0.01 * t) + widen(far[0, r, :]))
            trk[r, :] = 0.5 * (t + widen(far[1, r, :])) - old[r, :]

        ready.add("base")

    def keys_out():
        @pl.loop(0, 8)
        def _(i):
            n = toks // 8
            r = pl.ds(pl.multiple_of(i * n, n), n)
            keys[r, :] = acc[r, :].astype(BF16)

    loads["cot"].wait()
    pl.semaphore_wait(barrier, 4)
    issue("x", 0)
    for n, q in enumerate((0, 2, 1, 3)):
        loads[q].wait()
        w[0, q] = par[:, col(q)].astype(BF16)
        issue("pmpm"[n], n // 2)
    for i in range(1, DEPTH):
        issue("x", i)
    loads["tok"].wait()

    jobs = [
        (0.1, send_pair),
        (0.6, lambda: use(0)),
        (4.2, lambda: use(1)),
        (4.6, lambda: use(3)),
        (5.2, lambda: (sums(2, 0), sums(2, 1))),
        (6.7, lambda: use(2)),
        (9.3, average),
        (9.4, lambda: use(4)),
        (9.6, lambda: (own_sum(0, True, False), own_sum(1, True, False))),
        (10.1, lambda: sums(1, 0)),
        (10.9, lambda: sums(3, 0)),
        (12.1, lambda: sums(1, 1)),
        (12.3, lambda: use(5)),
        (13.3, lambda: sums(3, 1)),
        (13.4, lambda: use(7)),
        (15.3, lambda: (use(6), keys_out())),
        (16.1, lambda: own_sum(0, False, True)),
        (16.3, lambda: (add_finished(0), add_finished(1), add_finished(2))),
    ]
    started = {"x": DEPTH, "p": 2, "m": 2}
    order = [(key, 0, name, i) for key, name, i in program if i >= started[name]]
    order += [(key, 1, "", job) for key, job in jobs]
    for key, kind, name, what in sorted(order, key=lambda e: e[:3]):
        if kind:
            what()
        else:
            issue(name, what)
    own_sum(1, False, True)
    add_finished(3)
    add_finished(4)

    for name, items in links.items():
        for tag, c in items:
            if tag not in seen:
                seen.add(tag)
                c.wait_recv()
        for tag, c in items[-DEPTH:]:
            c.wait_send()
    for c in pair:
        c.wait_send()


def write_out(keys, back, par, trk, keys_h, back_h, par_h, trk_h, done):
    copies = []
    for src, dst in ((back, back_h), (par, par_h), (trk, trk_h), (keys, keys_h)):
        n = src.shape[0] // 4
        for i in range(4):
            r = pl.ds(i * n, n)
            copies.append(pltpu.make_async_copy(src.at[r], dst.at[0, r], done.at[len(copies)]))
    for c in copies:
        c.start()
    for c in copies:
        c.wait()


def call(level, tokens, cotangent, params, tracker, grad_old):
    _, toks, d = tokens.shape
    _, rows, kv = params.shape
    wide = kv // Q
    scale = 1.0 / float(toks * 2 * NZ) ** 0.5
    sem = pltpu.SemaphoreType.DMA
    hbm = pl.BlockSpec(memory_space=pltpu.HBM)
    vmem = pl.BlockSpec(memory_space=pltpu.VMEM)
    results = pl.pallas_call(
        functools.partial(kernel, level, scale),
        out_shape=(
            pltpu.VMEM((toks, kv), BF16),
            pltpu.VMEM((toks, d), BF16),
            pltpu.VMEM((rows, kv), F32),
            pltpu.VMEM((rows, kv), F32),
        ),
        in_specs=[hbm] * 5,
        out_specs=(vmem,) * 4,
        scratch_shapes=[
            pltpu.VMEM((toks, d), BF16),
            pltpu.VMEM((toks, kv), BF16),
            pltpu.VMEM((rows, kv), F32),
            pltpu.VMEM((8, Q, rows, wide), BF16),
            pltpu.VMEM((3, rows, kv), BF16),
            pltpu.VMEM((NZ, toks, rows), BF16),
            pltpu.VMEM((toks, kv), BF16),
            pltpu.VMEM((2, rows // 2, kv), BF16),
            pltpu.VMEM((2, rows, kv), BF16),
            pltpu.VMEM((2, rows, kv), BF16),
            pltpu.VMEM((2, rows, kv), BF16),
            pltpu.VMEM((toks, kv), F32),
            sem((Q + 4,)),
            sem((16,)), sem((16,)), sem((18,)), sem((18,)), sem((18,)), sem((18,)), sem((2,)), sem((2,)),
        ],
        compiler_params=pltpu.CompilerParams(
            collective_id=level, has_side_effects=True, vmem_limit_bytes=50 << 20
        ),
        cost_estimate=pl.CostEstimate(
            flops=6 * toks * d * kv, bytes_accessed=14 << 20, transcendentals=0
        ),
        name=f"train_step_{level}",
    )(tokens, cotangent, params, tracker, grad_old)
    return pl.pallas_call(
        write_out,
        out_shape=(
            jax.ShapeDtypeStruct(cotangent.shape, BF16),
            jax.ShapeDtypeStruct(tokens.shape, BF16),
            jax.ShapeDtypeStruct(params.shape, F32),
            jax.ShapeDtypeStruct(params.shape, F32),
        ),
        in_specs=[vmem] * 4,
        out_specs=(hbm,) * 4,
        scratch_shapes=[sem((16,))],
        compiler_params=pltpu.CompilerParams(vmem_limit_bytes=1 << 20),
        name="write_out",
    )(*[pltpu.with_memory_space_constraint(r, pltpu.VMEM) for r in results])


def on_device(tokens, cotangent, params, tracker, grad_old, step):
    branches = [functools.partial(call, level) for level in range(3)]
    return lax.switch(
        jnp.clip(step[0], 0, 2), branches, tokens, cotangent, params, tracker, grad_old
    )


def solution(mesh):
    rows = P("rep", "tp", None)
    return jax.shard_map(
        on_device,
        mesh=mesh,
        in_specs=(rows,) * 5 + (P(),),
        out_specs=(rows,) * 4,
        check_vma=False,
    )
```

```python
import functools

import jax
import jax.numpy as jnp
from jax import lax
from jax.experimental import pallas as pl
from jax.experimental.pallas import tpu as pltpu
from jax.sharding import PartitionSpec as P

MESH = pl.DeviceIdType.MESH
Q = 4
NZ = 4
DEPTH = 3
F32, BF16 = jnp.float32, jnp.bfloat16
NT = (((1,), (1,)), ((), ()))
TN = (((0,), (0,)), ((), ()))


def kernel(
    level, scale,
    tok_h, cot_h, par_h, trk_h, old_h,
    keys, back, par, trk,
    tok, cot, old, w, part, tokp, cotp, rx, zf, mine, far, acc, accp, backp, keysp, keysi,
    load, xs, xr, ps, pr, ms, mr, fs, fr,
):
    rep, tp = lax.axis_index("rep"), lax.axis_index("tp")
    line, z = lax.div(tp, NZ), lax.rem(tp, NZ)
    toks = tok.shape[0]
    rows, kv = par.shape
    wide = kv // Q
    stride = 2**level
    bit = lax.rem(lax.div(rep, stride), 2)
    step = 1 - 2 * lax.rem(z + rep, 2)
    zp, zi = lax.rem(z + step + NZ, NZ), lax.rem(z - step + NZ, NZ)
    twin = (rep, lax.rem(tp + NZ, 2 * NZ))
    pal = (rep, line * NZ + zp)
    near = (rep, line * NZ + zi)
    partner = (rep + stride * (1 - 2 * bit), tp)

    def col(q):
        return pl.ds(q * wide, wide)

    def cols_of(slot, pals=False):
        a, b = (zp, lax.rem(z + 2, NZ)) if pals else (z, zi)
        owner = lax.rem(line + slot // 2, 2) * NZ + (b if slot % 2 else a)
        return pl.ds(pl.multiple_of(owner * rows, 128), rows)

    barrier = pltpu.get_barrier_semaphore()
    for other in (twin, pal, near, partner):
        pl.semaphore_signal(barrier, 1, device_id=other, device_id_type=MESH)
    loads = {"cot": pltpu.make_async_copy(cot_h.at[0], cot, load.at[0])}
    for q in range(Q):
        loads[q] = pltpu.make_async_copy(par_h.at[0, :, col(q)], par.at[:, col(q)], load.at[1 + q])
    loads["tok"] = pltpu.make_async_copy(tok_h.at[0], tok, load.at[Q + 1])
    loads["trk"] = pltpu.make_async_copy(trk_h.at[0], trk, load.at[Q + 2])
    loads["old"] = pltpu.make_async_copy(old_h.at[0], old, load.at[Q + 3])
    for c in loads.values():
        c.start()

    half, n4 = toks // 2, rows // 4
    cut = rows // 2
    lo, hi = pl.ds(0, cut), pl.ds(cut, rows - cut)

    def quarter(i):
        return pl.ds(i * n4, n4)

    def halves(i):
        return pl.ds(i * half, half)

    xl = [(("w", 2, q), 0.0, w.at[0, q], w.at[2, q]) for q in range(Q)]
    xl += [(("w", 3, q), q + 1.2, w.at[1, q], w.at[3, q]) for q in range(3)]
    xl += [(("w", 3, 3), 4.2, w.at[1, 3, lo], w.at[3, 3, lo])]
    xl += [(("rx", 1, i), 5.2, part.at[2, quarter(i)], rx.at[1, quarter(i)]) for i in range(4)]
    xl += [(("rx", 0, i), 6.1, part.at[1, quarter(i)], rx.at[0, quarter(i)]) for i in range(4)]
    xend = [1, 2, 3, 4, 5, 6, 7, 7.5, 8.5, 9.5, 10.5, 11.5, 12.5, 13.5, 14.5, 15.5]
    pp = [(("c", 0, i), 0.0, cot.at[halves(i)], cotp.at[halves(i)]) for i in (0, 1)]
    pp += [(("t", s, 0), 0.1, tok.at[:, cols_of(s, True)], tokp.at[s]) for s in (3, 2, 1, 0)]
    pp += [(("b", s, 0), t, backp.at[s], back.at[:, cols_of(s)]) for s, t in ((0, 3.7), (1, 4.7), (2, 4.8))]
    pp += [(("k", 0, 0), 9.0, keysp, keysi)]
    pp += [(("b", 3, 0), 8.5, backp.at[3], back.at[:, cols_of(3)])]
    pend = [1.6, 3.2, 4.6, 5.6, 6.6, 7.6, 8.6, 9.6, 10.6, 13.4, 15.4]
    ml = [(("w", 1, q), 0.0, w.at[0, q], w.at[1, q]) for q in range(Q)]
    ml += [(("v", 3, 3), 4.3, w.at[2, 3, hi], w.at[3, 3, hi])]
    ml += [(("zf", 0, i), 8.7 + i, part.at[0, quarter(i)], zf.at[quarter(i)]) for i in range(4)]
    mend = [1, 2, 3, 4, 4.8, 9.7, 10.7, 11.7, 12.7]
    links, arrives, program = {}, {}, []
    for name, items, ends, dev, ssem, rsem in (
        ("x", xl, xend, twin, xs, xr), ("p", pp, pend, pal, ps, pr), ("m", ml, mend, near, ms, mr),
    ):
        links[name] = []
        for i, (tag, made, src, dst) in enumerate(items):
            c = pltpu.make_async_remote_copy(
                src, dst, ssem.at[i], rsem.at[i], device_id=dev, device_id_type=MESH
            )
            links[name].append((tag, c))
            arrives[tag] = c
            free = ends[i - DEPTH] if i >= DEPTH else 0.0
            program.append((max(free, made), name, i))
    pair = [
        pltpu.make_async_remote_copy(
            mine.at[i], far.at[i], fs.at[i], fr.at[i], device_id=partner, device_id_type=MESH
        )
        for i in range(2)
    ]
    seen, ready = set(), set()

    def need(*tag):
        if tag not in seen:
            seen.add(tag)
            arrives[tag].wait_recv()

    def widen(x):
        return x.astype(F32)

    def prepare(link, tag):
        kind, j, q = tag
        if kind == "w" and j == 3:
            need("w", 1, q)
        if kind == "v":
            need("w", 2, q)
        if kind == "rx":
            assert ("sums", 2 + j) in ready
        if kind == "b":
            assert ("back", j) in ready
        if kind == "k":
            assert "keys" in ready
        if kind == "zf":
            assert ("sums", 1) in ready
            need("rx", 1, q)

            @pl.loop(0, n4 // 32)
            def _(m):
                r = pl.ds(pl.multiple_of(q * n4 + m * 32, 32), 32)
                part[0, r, :] = (widen(part[0, r, :]) + widen(rx[1, r, :])).astype(BF16)

    def issue(link, i):
        tag, c = links[link][i]
        if i >= DEPTH:
            links[link][i - DEPTH][1].wait_send()
        prepare(link, tag)
        c.start()

    def sums(slot):
        need("c", 0, 0)
        need("c", 0, 1)
        need("t", slot, 0)
        c = cols_of(slot)
        if slot == 0:
            assert "base" in ready

        @pl.loop(0, Q)
        def _(q):
            qc = pl.ds(pl.multiple_of(q * wide, 128), wide)
            g = lax.dot_general(tok[:, c], cot[:, qc], TN, preferred_element_type=F32)
            g = g + lax.dot_general(tokp[slot], cotp[:, qc], TN, preferred_element_type=F32)
            if slot:
                part[slot - 1, :, qc] = (g * scale).astype(BF16)
            else:
                trk[:, qc] += g * scale

        ready.add(("sums", slot))

    def add_rows(kind, i):
        assert "base" in ready
        need(kind, 0, i)
        src = rx.at[0] if kind == "rx" else zf

        @pl.loop(0, n4 // 32)
        def _(m):
            r = pl.ds(pl.multiple_of(i * n4 + m * 32, 32), 32)
            trk[r, :] += widen(src[r, :])

    def weights(slot):
        if slot:
            for q in range(Q):
                need("w", slot, q)
        if slot == 3:
            need("v", 3, 3)

    def grad_of(c_ref, slot, store):
        @pl.loop(0, 2)
        def _(m):
            r = pl.ds(pl.multiple_of(m * half, half), half)
            t = lax.dot_general(c_ref[r, col(0)], w[slot, 0], NT, preferred_element_type=F32)
            for q in range(1, Q):
                t = t + lax.dot_general(c_ref[r, col(q)], w[slot, q], NT, preferred_element_type=F32)
            store(r, t.astype(BF16))

    def keys_of(total, slot, read):
        @pl.loop(0, Q)
        def _(q):
            qc = pl.ds(pl.multiple_of(q * wide, 128), wide)
            t = jnp.dot(read(), w[slot, q], preferred_element_type=F32)
            if slot == 0:
                total[:, qc] = t
            else:
                total[:, qc] += t

    def own(slot):
        weights(slot)
        c = cols_of(slot)
        keys_of(acc, slot, lambda: tok[:, c])

        def store(r, v):
            back[r, c] = v

        grad_of(cot, slot, store)

    def pals_back(slot):
        weights(slot)
        need("c", 0, 0)
        need("c", 0, 1)

        def store(r, v):
            backp[slot, r, :] = v

        grad_of(cotp, slot, store)
        ready.add(("back", slot))

    def pals_keys(slot):
        weights(slot)
        need("t", slot, 0)
        keys_of(accp, slot, lambda: tokp[slot])

    def by_rows(f):
        n = toks // 8

        @pl.loop(0, 8)
        def _(i):
            f(pl.ds(pl.multiple_of(i * n, n), n))

    def pals_keys_out():
        def f(r):
            keysp[r, :] = accp[r, :].astype(BF16)

        by_rows(f)
        ready.add("keys")

    def keys_out():
        need("k", 0, 0)

        def f(r):
            keys[r, :] = (acc[r, :] + widen(keysi[r, :])).astype(BF16)

        by_rows(f)

    def send_pair():
        loads["trk"].wait()

        @pl.loop(0, rows // 32)
        def _(i):
            r = pl.ds(pl.multiple_of(i * 32, 32), 32)
            t = trk[r, :]
            mine[0, r, :] = (par[r, :] - 0.01 * t).astype(BF16)
            mine[1, r, :] = t.astype(BF16)

        pair[0].start()
        pair[1].start()

    def average():
        loads["old"].wait()
        pair[0].wait_recv()
        pair[1].wait_recv()

        @pl.loop(0, rows // 32)
        def _(i):
            r = pl.ds(pl.multiple_of(i * 32, 32), 32)
            t = trk[r, :]
            par[r, :] = 0.5 * ((par[r, :] - 0.01 * t) + widen(far[0, r, :]))
            trk[r, :] = 0.5 * (t + widen(far[1, r, :])) - old[r, :]

        ready.add("base")

    def cast(q):
        loads[q].wait()
        w[0, q] = par[:, col(q)].astype(BF16)

    loads["cot"].wait()
    cast(0)
    pl.semaphore_wait(barrier, 4)
    issue("p", 0)
    issue("x", 0)
    issue("m", 0)
    issue("p", 1)
    for q in range(1, Q):
        cast(q)
        if q < DEPTH:
            issue("x", q)
            issue("m", q)
    loads["tok"].wait()

    jobs = [
        (0.1, send_pair),
        (0.6, lambda: own(0)),
        (3.5, lambda: pals_back(0)),
        (4.3, lambda: pals_back(1)),
        (4.6, lambda: pals_back(2)),
        (4.9, lambda: sums(3)),
        (5.8, lambda: sums(2)),
        (6.3, lambda: own(1)),
        (6.7, lambda: sums(1)),
        (7.1, lambda: own(2)),
        (7.7, lambda: (pals_keys(0), pals_keys(1), pals_keys(2))),
        (8.1, lambda: (pals_back(3), pals_keys(3), pals_keys_out())),
        (9.2, average),
        (9.3, lambda: sums(0)),
        (10.0, lambda: own(3)),
        (12.7, lambda: add_rows("rx", 0)),
        (13.5, lambda: (add_rows("zf", 0), add_rows("zf", 1))),
        (13.7, lambda: (add_rows("rx", 1), add_rows("zf", 2), add_rows("zf", 3))),
        (14.6, keys_out),
        (14.7, lambda: add_rows("rx", 2)),
    ]
    started = {"x": DEPTH, "p": 2, "m": DEPTH}
    order = [(key, 0, name, i) for key, name, i in program if i >= started[name]]
    order += [(key, 1, "", job) for key, job in jobs]
    for key, kind, name, what in sorted(order, key=lambda e: e[:3]):
        if kind:
            what()
        else:
            issue(name, what)
    add_rows("rx", 3)

    for name, items in links.items():
        for tag, c in items:
            if tag not in seen:
                seen.add(tag)
                c.wait_recv()
        for tag, c in items[-DEPTH:]:
            c.wait_send()
    for c in pair:
        c.wait_send()


def write_out(keys, back, par, trk, keys_h, back_h, par_h, trk_h, done):
    copies = []
    for src, dst in ((back, back_h), (par, par_h), (trk, trk_h), (keys, keys_h)):
        n = src.shape[0] // 4
        for i in range(4):
            r = pl.ds(i * n, n)
            copies.append(pltpu.make_async_copy(src.at[r], dst.at[0, r], done.at[len(copies)]))
    for c in copies:
        c.start()
    for c in copies:
        c.wait()


def call(level, tokens, cotangent, params, tracker, grad_old):
    _, toks, d = tokens.shape
    _, rows, kv = params.shape
    wide = kv // Q
    scale = 1.0 / float(toks * 2 * NZ) ** 0.5
    sem = pltpu.SemaphoreType.DMA
    hbm = pl.BlockSpec(memory_space=pltpu.HBM)
    vmem = pl.BlockSpec(memory_space=pltpu.VMEM)
    results = pl.pallas_call(
        functools.partial(kernel, level, scale),
        out_shape=(
            pltpu.VMEM((toks, kv), BF16),
            pltpu.VMEM((toks, d), BF16),
            pltpu.VMEM((rows, kv), F32),
            pltpu.VMEM((rows, kv), F32),
        ),
        in_specs=[hbm] * 5,
        out_specs=(vmem,) * 4,
        scratch_shapes=[
            pltpu.VMEM((toks, d), BF16),
            pltpu.VMEM((toks, kv), BF16),
            pltpu.VMEM((rows, kv), F32),
            pltpu.VMEM((4, Q, rows, wide), BF16),
            pltpu.VMEM((3, rows, kv), BF16),
            pltpu.VMEM((4, toks, rows), BF16),
            pltpu.VMEM((toks, kv), BF16),
            pltpu.VMEM((2, rows, kv), BF16),
            pltpu.VMEM((rows, kv), BF16),
            pltpu.VMEM((2, rows, kv), BF16),
            pltpu.VMEM((2, rows, kv), BF16),
            pltpu.VMEM((toks, kv), F32),
            pltpu.VMEM((toks, kv), F32),
            pltpu.VMEM((4, toks, rows), BF16),
            pltpu.VMEM((toks, kv), BF16),
            pltpu.VMEM((toks, kv), BF16),
            sem((Q + 4,)),
            sem((16,)), sem((16,)), sem((11,)), sem((11,)), sem((9,)), sem((9,)), sem((2,)), sem((2,)),
        ],
        compiler_params=pltpu.CompilerParams(
            collective_id=level, has_side_effects=True, vmem_limit_bytes=50 << 20
        ),
        cost_estimate=pl.CostEstimate(
            flops=6 * toks * d * kv, bytes_accessed=14 << 20, transcendentals=0
        ),
        name=f"train_step_{level}",
    )(tokens, cotangent, params, tracker, grad_old)
    return pl.pallas_call(
        write_out,
        out_shape=(
            jax.ShapeDtypeStruct(cotangent.shape, BF16),
            jax.ShapeDtypeStruct(tokens.shape, BF16),
            jax.ShapeDtypeStruct(params.shape, F32),
            jax.ShapeDtypeStruct(params.shape, F32),
        ),
        in_specs=[vmem] * 4,
        out_specs=(hbm,) * 4,
        scratch_shapes=[sem((16,))],
        compiler_params=pltpu.CompilerParams(vmem_limit_bytes=1 << 20),
        name="write_out",
    )(*[pltpu.with_memory_space_constraint(r, pltpu.VMEM) for r in results])


def on_device(tokens, cotangent, params, tracker, grad_old, step):
    branches = [functools.partial(call, level) for level in range(3)]
    return lax.switch(
        step[0], branches, tokens, cotangent, params, tracker, grad_old
    )


def solution(mesh):
    rows = P("rep", "tp", None)
    return jax.shard_map(
        on_device,
        mesh=mesh,
        in_specs=(rows,) * 5 + (P(),),
        out_specs=(rows,) * 4,
        check_vma=False,
    )
```

```python
import functools

import jax
import jax.numpy as jnp
from jax import lax
from jax.experimental import pallas as pl
from jax.experimental.pallas import tpu as pltpu
from jax.sharding import PartitionSpec as P

MESH = pl.DeviceIdType.MESH
Q = 4
NZ = 4
DEPTH = 3
F32, BF16 = jnp.float32, jnp.bfloat16
NT = (((1,), (1,)), ((), ()))
TN = (((0,), (0,)), ((), ()))


def kernel(
    scale,
    tok_h, cot_h, par_h, trk_h, old_h, step_h,
    keys, back, par, trk,
    tok, cot, old, w, part, tokp, cotp, rx, zf, mine, far, acc, accp, backp, keysp, keysi,
    which, load, xs, xr, ps, pr, ms, mr, ys, yr, fs, fr, cs, cr,
):
    rep, tp = lax.axis_index("rep"), lax.axis_index("tp")
    line, z = lax.div(tp, NZ), lax.rem(tp, NZ)
    toks = tok.shape[0]
    rows, kv = par.shape
    wide = kv // Q
    step = 1 - 2 * lax.rem(z + rep, 2)
    zp, zi = lax.rem(z + step + NZ, NZ), lax.rem(z - step + NZ, NZ)
    twin = (rep, lax.rem(tp + NZ, 2 * NZ))
    pal = (rep, line * NZ + zp)
    near = (rep, line * NZ + zi)
    y = lax.rem(lax.div(rep, 2), 4)
    mate = (rep + 1 - 2 * lax.rem(rep, 2), tp)
    beside = (rep + 2 * (1 - 2 * lax.rem(y, 2)), tp)
    across = (rep + 2 * (3 - 2 * y), tp)

    def col(q):
        return pl.ds(q * wide, wide)

    def cols_of(slot, pals=False):
        a, b = (zp, lax.rem(z + 2, NZ)) if pals else (z, zi)
        owner = lax.rem(line + slot // 2, 2) * NZ + (b if slot % 2 else a)
        return pl.ds(pl.multiple_of(owner * rows, 128), rows)

    loads = {"cot": pltpu.make_async_copy(cot_h.at[0], cot, load.at[0])}
    for q in range(Q):
        loads[q] = pltpu.make_async_copy(par_h.at[0, :, col(q)], par.at[:, col(q)], load.at[1 + q])
    loads["tok"] = pltpu.make_async_copy(tok_h.at[0], tok, load.at[Q + 1])
    loads["trk"] = pltpu.make_async_copy(trk_h.at[0], trk, load.at[Q + 2])
    loads["old"] = pltpu.make_async_copy(old_h.at[0], old, load.at[Q + 3])
    loads["step"] = pltpu.make_async_copy(step_h, which, load.at[Q + 4])
    loads[0].start()
    loads["cot"].start()
    barrier = pltpu.get_barrier_semaphore()
    for other in (twin, pal, near, mate, beside, across):
        pl.semaphore_signal(barrier, 1, device_id=other, device_id_type=MESH)

    half, n4 = toks // 2, rows // 4
    cut = rows // 2
    lo, hi = pl.ds(0, cut), pl.ds(cut, rows - cut)

    def quarter(i):
        return pl.ds(i * n4, n4)

    def halves(i):
        return pl.ds(i * half, half)

    xl = [(("w", 2, q), 0.0, w.at[0, q], w.at[2, q]) for q in range(Q)]
    xl += [(("w", 3, q), q + 1.2, w.at[1, q], w.at[3, q]) for q in range(3)]
    xl += [(("w", 3, 3), 4.2, w.at[1, 3, lo], w.at[3, 3, lo])]
    xl += [(("rx", 1, i), 5.2, part.at[2, quarter(i)], rx.at[1, quarter(i)]) for i in range(4)]
    xl += [(("rx", 0, i), 6.1, part.at[1, quarter(i)], rx.at[0, quarter(i)]) for i in range(4)]
    xend = [1, 2, 3, 4, 5, 6, 7, 7.5, 8.5, 9.5, 10.5, 11.5, 12.5, 13.5, 14.5, 15.5]
    pp = [(("c", 0, i), 0.0, cot.at[halves(i)], cotp.at[halves(i)]) for i in (0, 1)]
    pp += [(("t", s, 0), 0.1, tok.at[:, cols_of(s, True)], tokp.at[s]) for s in (3, 2, 1, 0)]
    pp += [(("b", s, 0), t, backp.at[s], back.at[:, cols_of(s)]) for s, t in ((0, 3.7), (1, 4.7), (2, 4.8))]
    pp += [(("k", 0, 0), 9.0, keysp, keysi)]
    pp += [(("b", 3, 0), 8.5, backp.at[3], back.at[:, cols_of(3)])]
    pend = [1.6, 3.2, 4.6, 5.6, 6.6, 7.6, 8.6, 9.6, 10.6, 13.4, 15.4]
    ml = [(("w", 1, q), 0.0, w.at[0, q], w.at[1, q]) for q in range(Q)]
    ml += [(("v", 3, 3), 4.3, w.at[2, 3, hi], w.at[3, 3, hi])]
    ml += [(("zf", 0, i), 8.7 + i, part.at[0, quarter(i)], zf.at[quarter(i)]) for i in range(4)]
    mend = [1, 2, 3, 4, 4.8, 9.7, 10.7, 11.7, 12.7]
    both = [(a, i) for a in range(2) for i in range(4)]
    yl = [(("y", a, i), 0.15, mine.at[a, quarter(i)], far.at[1, a, quarter(i)]) for a, i in both]
    yend = [n + 1.2 for n in range(8)]
    fl = [
        (("f", a, i), 4 * a + i + 1.4, far.at[1, a, quarter(i)], far.at[2, a, quarter(i)])
        for a, i in both
    ]
    fend = [n + 2.4 for n in range(8)]
    cl = [(("o", a, 0), 0.15, mine.at[a], far.at[0, a]) for a in range(2)]
    links, arrives, program = {}, {}, []
    for name, items, ends, dev, ssem, rsem in (
        ("x", xl, xend, twin, xs, xr), ("p", pp, pend, pal, ps, pr), ("m", ml, mend, near, ms, mr),
        ("y", yl, yend, beside, ys, yr), ("f", fl, fend, across, fs, fr), ("o", cl, [1, 2], mate, cs, cr),
    ):
        links[name] = []
        for i, (tag, made, src, dst) in enumerate(items):
            c = pltpu.make_async_remote_copy(
                src, dst, ssem.at[i], rsem.at[i], device_id=dev, device_id_type=MESH
            )
            links[name].append((tag, c))
            arrives[tag] = c
            free = ends[i - DEPTH] if i >= DEPTH else 0.0
            program.append((max(free, made), name, i))
    seen, ready = set(), set()

    def need(*tag):
        if tag not in seen:
            seen.add(tag)
            arrives[tag].wait_recv()

    def widen(x):
        return x.astype(F32)

    def prepare(link, tag):
        kind, j, q = tag
        if kind == "w" and j == 3:
            need("w", 1, q)
        if kind == "v":
            need("w", 2, q)
        if kind == "rx":
            assert ("sums", 2 + j) in ready
        if kind == "b":
            assert ("back", j) in ready
        if kind in ("y", "o"):
            assert "mine" in ready
        if kind == "f":
            need("y", j, q)
        if kind == "k":
            assert "keys" in ready
        if kind == "zf":
            assert ("sums", 1) in ready
            need("rx", 1, q)

            @pl.loop(0, n4 // 32)
            def _(m):
                r = pl.ds(pl.multiple_of(q * n4 + m * 32, 32), 32)
                part[0, r, :] = (widen(part[0, r, :]) + widen(rx[1, r, :])).astype(BF16)

    def issue(link, i):
        tag, c = links[link][i]
        if i >= DEPTH:
            links[link][i - DEPTH][1].wait_send()
        prepare(link, tag)
        c.start()

    def sums(slot):
        need("c", 0, 0)
        need("c", 0, 1)
        need("t", slot, 0)
        c = cols_of(slot)
        if slot == 0:
            assert "base" in ready

        @pl.loop(0, Q)
        def _(q):
            qc = pl.ds(pl.multiple_of(q * wide, 128), wide)
            g = lax.dot_general(tok[:, c], cot[:, qc], TN, preferred_element_type=F32)
            g = g + lax.dot_general(tokp[slot], cotp[:, qc], TN, preferred_element_type=F32)
            if slot:
                part[slot - 1, :, qc] = (g * scale).astype(BF16)
            else:
                trk[:, qc] += g * scale

        ready.add(("sums", slot))

    def add_rows(kind, i):
        assert "base" in ready
        need(kind, 0, i)
        src = rx.at[0] if kind == "rx" else zf

        @pl.loop(0, n4 // 32)
        def _(m):
            r = pl.ds(pl.multiple_of(i * n4 + m * 32, 32), 32)
            trk[r, :] += widen(src[r, :])

    def weights(slot):
        if slot:
            for q in range(Q):
                need("w", slot, q)
        if slot == 3:
            need("v", 3, 3)

    def grad_of(c_ref, slot, store):
        @pl.loop(0, 2)
        def _(m):
            r = pl.ds(pl.multiple_of(m * half, half), half)
            t = lax.dot_general(c_ref[r, col(0)], w[slot, 0], NT, preferred_element_type=F32)
            for q in range(1, Q):
                t = t + lax.dot_general(c_ref[r, col(q)], w[slot, q], NT, preferred_element_type=F32)
            store(r, t.astype(BF16))

    def keys_of(total, slot, read):
        @pl.loop(0, Q)
        def _(q):
            qc = pl.ds(pl.multiple_of(q * wide, 128), wide)
            t = jnp.dot(read(), w[slot, q], preferred_element_type=F32)
            if slot == 0:
                total[:, qc] = t
            else:
                total[:, qc] += t

    def own(slot):
        weights(slot)
        c = cols_of(slot)
        keys_of(acc, slot, lambda: tok[:, c])

        def store(r, v):
            back[r, c] = v

        grad_of(cot, slot, store)

    def pals_back(slot):
        weights(slot)
        need("c", 0, 0)
        need("c", 0, 1)

        def store(r, v):
            backp[slot, r, :] = v

        grad_of(cotp, slot, store)
        ready.add(("back", slot))

    def pals_keys(slot):
        weights(slot)
        need("t", slot, 0)
        keys_of(accp, slot, lambda: tokp[slot])

    def by_rows(f):
        n = toks // 8

        @pl.loop(0, 8)
        def _(i):
            f(pl.ds(pl.multiple_of(i * n, n), n))

    def pals_keys_out():
        def f(r):
            keysp[r, :] = accp[r, :].astype(BF16)

        by_rows(f)
        ready.add("keys")

    def keys_out():
        need("k", 0, 0)

        def f(r):
            keys[r, :] = (acc[r, :] + widen(keysi[r, :])).astype(BF16)

        by_rows(f)

    def send_pair():
        loads["trk"].wait()

        @pl.loop(0, rows // 32)
        def _(i):
            r = pl.ds(pl.multiple_of(i * 32, 32), 32)
            t = trk[r, :]
            mine[0, r, :] = (par[r, :] - 0.01 * t).astype(BF16)
            mine[1, r, :] = t.astype(BF16)

        ready.add("mine")

    def average():
        loads["old"].wait()
        loads["step"].wait()
        for a, i in both:
            need("y", a, i)
            need("f", a, i)
        need("o", 0, 0)
        need("o", 1, 0)
        k = which[0]
        one = [
            jnp.where(k <= 0, 1.0, 0.0), jnp.where(k == 1, 1.0, 0.0), jnp.where(k >= 2, 1.0, 0.0),
        ]

        def partners(a, r):
            t = one[0] * widen(far[0, a, r, :]) + one[1] * widen(far[1, a, r, :])
            return t + one[2] * widen(far[2, a, r, :])

        @pl.loop(0, rows // 32)
        def _(i):
            r = pl.ds(pl.multiple_of(i * 32, 32), 32)
            t = trk[r, :]
            par[r, :] = 0.5 * ((par[r, :] - 0.01 * t) + partners(0, r))
            trk[r, :] = 0.5 * (t + partners(1, r)) - old[r, :]

        ready.add("base")

    def cast(q):
        loads[q].wait()
        w[0, q] = par[:, col(q)].astype(BF16)

    cast(0)
    pl.semaphore_wait(barrier, 6)
    issue("x", 0)
    issue("m", 0)
    loads["cot"].wait()
    issue("p", 0)
    issue("p", 1)
    for name in (1, 2, 3, "trk", "tok", "old", "step"):
        loads[name].start()
    for q in range(1, Q):
        cast(q)
        if q < DEPTH:
            issue("x", q)
            issue("m", q)
    loads["tok"].wait()

    jobs = [
        (0.1, send_pair),
        (0.6, lambda: own(0)),
        (3.5, lambda: pals_back(0)),
        (4.3, lambda: pals_back(1)),
        (4.6, lambda: pals_back(2)),
        (4.9, lambda: sums(3)),
        (5.8, lambda: sums(2)),
        (6.3, lambda: own(1)),
        (6.7, lambda: sums(1)),
        (7.1, lambda: own(2)),
        (7.7, lambda: (pals_keys(0), pals_keys(1), pals_keys(2))),
        (8.1, lambda: (pals_back(3), pals_keys(3), pals_keys_out())),
        (9.2, lambda: own(3)),
        (11.2, average),
        (11.3, lambda: sums(0)),
        (12.7, lambda: add_rows("rx", 0)),
        (13.5, lambda: (add_rows("zf", 0), add_rows("zf", 1))),
        (13.7, lambda: (add_rows("rx", 1), add_rows("zf", 2), add_rows("zf", 3))),
        (14.6, keys_out),
        (14.7, lambda: add_rows("rx", 2)),
    ]
    started = {"x": DEPTH, "p": 2, "m": DEPTH, "y": 0, "f": 0, "o": 0}
    order = [(key, 0, name, i) for key, name, i in program if i >= started[name]]
    order += [(key, 1, "", job) for key, job in jobs]
    for key, kind, name, what in sorted(order, key=lambda e: e[:3]):
        if kind:
            what()
        else:
            issue(name, what)
    add_rows("rx", 3)

    for name, items in links.items():
        for tag, c in items:
            if tag not in seen:
                seen.add(tag)
                c.wait_recv()
        for tag, c in items[-DEPTH:]:
            c.wait_send()


def write_out(keys, back, par, trk, keys_h, back_h, par_h, trk_h, done):
    copies = []
    for src, dst in ((back, back_h), (par, par_h), (trk, trk_h), (keys, keys_h)):
        n = src.shape[0] // 2
        for i in range(2):
            r = pl.ds(i * n, n)
            copies.append(pltpu.make_async_copy(src.at[r], dst.at[0, r], done.at[len(copies)]))
    for c in copies:
        c.start()
    for c in copies:
        c.wait()


def on_device(tokens, cotangent, params, tracker, grad_old, step):
    _, toks, d = tokens.shape
    _, rows, kv = params.shape
    wide = kv // Q
    scale = 1.0 / float(toks * 2 * NZ) ** 0.5
    sem = pltpu.SemaphoreType.DMA
    hbm = pl.BlockSpec(memory_space=pltpu.HBM)
    vmem = pl.BlockSpec(memory_space=pltpu.VMEM)
    results = pl.pallas_call(
        functools.partial(kernel, scale),
        out_shape=(
            pltpu.VMEM((toks, kv), BF16),
            pltpu.VMEM((toks, d), BF16),
            pltpu.VMEM((rows, kv), F32),
            pltpu.VMEM((rows, kv), F32),
        ),
        in_specs=[hbm] * 6,
        out_specs=(vmem,) * 4,
        scratch_shapes=[
            pltpu.VMEM((toks, d), BF16),
            pltpu.VMEM((toks, kv), BF16),
            pltpu.VMEM((rows, kv), F32),
            pltpu.VMEM((4, Q, rows, wide), BF16),
            pltpu.VMEM((3, rows, kv), BF16),
            pltpu.VMEM((4, toks, rows), BF16),
            pltpu.VMEM((toks, kv), BF16),
            pltpu.VMEM((2, rows, kv), BF16),
            pltpu.VMEM((rows, kv), BF16),
            pltpu.VMEM((2, rows, kv), BF16),
            pltpu.VMEM((3, 2, rows, kv), BF16),
            pltpu.VMEM((toks, kv), F32),
            pltpu.VMEM((toks, kv), F32),
            pltpu.VMEM((4, toks, rows), BF16),
            pltpu.VMEM((toks, kv), BF16),
            pltpu.VMEM((toks, kv), BF16),
            pltpu.SMEM((1,), jnp.int32),
            sem((Q + 5,)),
            sem((16,)), sem((16,)), sem((11,)), sem((11,)), sem((9,)), sem((9,)),
            sem((8,)), sem((8,)), sem((8,)), sem((8,)), sem((2,)), sem((2,)),
        ],
        compiler_params=pltpu.CompilerParams(
            collective_id=0, has_side_effects=True, vmem_limit_bytes=50 << 20
        ),
        cost_estimate=pl.CostEstimate(
            flops=6 * toks * d * kv, bytes_accessed=14 << 20, transcendentals=0
        ),
        name="train_step",
    )(tokens, cotangent, params, tracker, grad_old, step)
    return pl.pallas_call(
        write_out,
        out_shape=(
            jax.ShapeDtypeStruct(cotangent.shape, BF16),
            jax.ShapeDtypeStruct(tokens.shape, BF16),
            jax.ShapeDtypeStruct(params.shape, F32),
            jax.ShapeDtypeStruct(params.shape, F32),
        ),
        in_specs=[vmem] * 4,
        out_specs=(hbm,) * 4,
        scratch_shapes=[sem((8,))],
        compiler_params=pltpu.CompilerParams(vmem_limit_bytes=1 << 20),
        name="write_out",
    )(*[pltpu.with_memory_space_constraint(r, pltpu.VMEM) for r in results])


def solution(mesh):
    rows = P("rep", "tp", None)
    return jax.shard_map(
        on_device,
        mesh=mesh,
        in_specs=(rows,) * 5 + (P(),),
        out_specs=(rows,) * 4,
        check_vma=False,
    )
```

```python
import functools

import jax
import jax.numpy as jnp
from jax import lax
from jax.experimental import pallas as pl
from jax.experimental.pallas import tpu as pltpu
from jax.sharding import PartitionSpec as P

MESH = pl.DeviceIdType.MESH
Q = 4
NZ = 4
DEPTH = 3
F32, BF16 = jnp.float32, jnp.bfloat16
NT = (((1,), (1,)), ((), ()))
TN = (((0,), (0,)), ((), ()))


def kernel(
    scale,
    tok_h, cot_h, par_h, trk_h, old_h, step_h,
    keys, back, par, trk,
    tok, cot, old, w, part, tokp, cotp, rx, zf, mine, far, acc, accp, backp, keysp, keysi,
    which, load, xs, xr, ps, pr, ms, mr, ys, yr, fs, fr, cs, cr,
):
    rep, tp = lax.axis_index("rep"), lax.axis_index("tp")
    line, z = lax.div(tp, NZ), lax.rem(tp, NZ)
    toks = tok.shape[0]
    rows, kv = par.shape
    wide = kv // Q
    step = 1 - 2 * lax.rem(z + rep, 2)
    zp, zi = lax.rem(z + step + NZ, NZ), lax.rem(z - step + NZ, NZ)
    twin = (rep, lax.rem(tp + NZ, 2 * NZ))
    pal = (rep, line * NZ + zp)
    near = (rep, line * NZ + zi)
    y = lax.rem(lax.div(rep, 2), 4)
    mate = (rep + 1 - 2 * lax.rem(rep, 2), tp)
    beside = (rep + 2 * (1 - 2 * lax.rem(y, 2)), tp)
    across = (rep + 2 * (3 - 2 * y), tp)

    def col(q):
        return pl.ds(q * wide, wide)

    def cols_of(slot, pals=False):
        a, b = (zp, lax.rem(z + 2, NZ)) if pals else (z, zi)
        owner = lax.rem(line + slot // 2, 2) * NZ + (b if slot % 2 else a)
        return pl.ds(pl.multiple_of(owner * rows, 128), rows)

    loads = {"cot": pltpu.make_async_copy(cot_h.at[0], cot, load.at[0])}
    for q in range(Q):
        loads[q] = pltpu.make_async_copy(par_h.at[0, :, col(q)], par.at[:, col(q)], load.at[1 + q])
    loads["tok"] = pltpu.make_async_copy(tok_h.at[0], tok, load.at[Q + 1])
    loads["trk"] = pltpu.make_async_copy(trk_h.at[0], trk, load.at[Q + 2])
    loads["old"] = pltpu.make_async_copy(old_h.at[0], old, load.at[Q + 3])
    loads["step"] = pltpu.make_async_copy(step_h, which, load.at[Q + 4])
    loads[0].start()
    loads["cot"].start()
    barrier = pltpu.get_barrier_semaphore()
    for other in (twin, pal, near, mate, beside, across):
        pl.semaphore_signal(barrier, 1, device_id=other, device_id_type=MESH)

    half, n4 = toks // 2, rows // 4
    cut = rows * 9 // 20
    lo, hi = pl.ds(0, cut), pl.ds(cut, rows - cut)

    def quarter(i):
        return pl.ds(i * n4, n4)

    def halves(i):
        return pl.ds(i * half, half)

    xl = [(("w", 2, q), 0.0, w.at[0, q], w.at[2, q]) for q in range(Q)]
    xl += [(("w", 3, q), q + 1.2, w.at[1, q], w.at[3, q]) for q in range(3)]
    xl += [(("w", 3, 3), 4.2, w.at[1, 3, lo], w.at[3, 3, lo])]
    xl += [(("rx", 1, i), 5.2, part.at[2, quarter(i)], rx.at[1, quarter(i)]) for i in range(4)]
    xl += [(("rx", 0, i), 6.1, part.at[1, quarter(i)], rx.at[0, quarter(i)]) for i in range(4)]
    xend = [1, 2, 3, 4, 5, 6, 7, 7.5, 8.5, 9.5, 10.5, 11.5, 12.5, 13.5, 14.5, 15.5]
    pp = [(("c", 0, i), 0.0, cot.at[halves(i)], cotp.at[halves(i)]) for i in (0, 1)]
    pp += [(("t", s, 0), 0.1, tok.at[:, cols_of(s, True)], tokp.at[s]) for s in (3, 2, 1, 0)]
    pp += [(("b", s, 0), t, backp.at[s], back.at[:, cols_of(s)]) for s, t in ((0, 3.7), (1, 4.7), (2, 4.8))]
    pp += [(("k", 0, 0), 9.0, keysp, keysi)]
    pp += [(("b", 3, 0), 8.5, backp.at[3], back.at[:, cols_of(3)])]
    pend = [1.6, 3.2, 4.6, 5.6, 6.6, 7.6, 8.6, 9.6, 10.6, 13.4, 15.4]
    ml = [(("w", 1, q), 0.0, w.at[0, q], w.at[1, q]) for q in range(Q)]
    ml += [(("v", 3, 3), 4.3, w.at[2, 3, hi], w.at[3, 3, hi])]
    ml += [(("zf", 0, i), 8.7 + i, part.at[0, quarter(i)], zf.at[quarter(i)]) for i in range(4)]
    mend = [1, 2, 3, 4, 4.8, 9.7, 10.7, 11.7, 12.7]
    both = [(a, i) for a in range(2) for i in range(4)]
    yl = [(("y", a, i), 0.15, mine.at[a, quarter(i)], far.at[1, a, quarter(i)]) for a, i in both]
    yend = [n + 1.2 for n in range(8)]
    fl = [
        (("f", a, i), 4 * a + i + 1.4, far.at[1, a, quarter(i)], far.at[2, a, quarter(i)])
        for a, i in both
    ]
    fend = [n + 2.4 for n in range(8)]
    cl = [(("o", a, 0), 0.15, mine.at[a], far.at[0, a]) for a in range(2)]
    links, arrives, program = {}, {}, []
    for name, items, ends, dev, ssem, rsem in (
        ("x", xl, xend, twin, xs, xr), ("p", pp, pend, pal, ps, pr), ("m", ml, mend, near, ms, mr),
        ("y", yl, yend, beside, ys, yr), ("f", fl, fend, across, fs, fr), ("o", cl, [1, 2], mate, cs, cr),
    ):
        links[name] = []
        for i, (tag, made, src, dst) in enumerate(items):
            c = pltpu.make_async_remote_copy(
                src, dst, ssem.at[i], rsem.at[i], device_id=dev, device_id_type=MESH
            )
            links[name].append((tag, c))
            arrives[tag] = c
            free = ends[i - DEPTH] if i >= DEPTH else 0.0
            program.append((max(free, made), name, i))
    seen, ready = set(), set()

    def need(*tag):
        if tag not in seen:
            seen.add(tag)
            arrives[tag].wait_recv()

    def widen(x):
        return x.astype(F32)

    def prepare(link, tag):
        kind, j, q = tag
        if kind == "w" and j == 3:
            need("w", 1, q)
        if kind == "v":
            need("w", 2, q)
        if kind == "rx":
            assert ("sums", 2 + j) in ready
        if kind == "b":
            assert ("back", j) in ready
        if kind in ("y", "o"):
            assert "mine" in ready
        if kind == "f":
            need("y", j, q)
        if kind == "k":
            assert "keys" in ready
        if kind == "zf":
            assert ("sums", 1) in ready
            need("rx", 1, q)

            @pl.loop(0, n4 // 32)
            def _(m):
                r = pl.ds(pl.multiple_of(q * n4 + m * 32, 32), 32)
                part[0, r, :] = (widen(part[0, r, :]) + widen(rx[1, r, :])).astype(BF16)

    def issue(link, i):
        tag, c = links[link][i]
        if i >= DEPTH:
            links[link][i - DEPTH][1].wait_send()
        prepare(link, tag)
        c.start()

    def sums(slot):
        need("c", 0, 0)
        need("c", 0, 1)
        need("t", slot, 0)
        c = cols_of(slot)
        if slot == 0:
            assert "base" in ready

        @pl.loop(0, Q)
        def _(q):
            qc = pl.ds(pl.multiple_of(q * wide, 128), wide)
            g = lax.dot_general(tok[:, c], cot[:, qc], TN, preferred_element_type=F32)
            g = g + lax.dot_general(tokp[slot], cotp[:, qc], TN, preferred_element_type=F32)
            if slot:
                part[slot - 1, :, qc] = (g * scale).astype(BF16)
            else:
                trk[:, qc] += g * scale

        ready.add(("sums", slot))

    def add_rows(kind, i):
        assert "base" in ready
        need(kind, 0, i)
        src = rx.at[0] if kind == "rx" else zf

        @pl.loop(0, n4 // 32)
        def _(m):
            r = pl.ds(pl.multiple_of(i * n4 + m * 32, 32), 32)
            trk[r, :] += widen(src[r, :])

    def weights(slot):
        if slot:
            for q in range(Q):
                need("w", slot, q)
        if slot == 3:
            need("v", 3, 3)

    def grad_of(c_ref, slot, store):
        @pl.loop(0, 2)
        def _(m):
            r = pl.ds(pl.multiple_of(m * half, half), half)
            t = lax.dot_general(c_ref[r, col(0)], w[slot, 0], NT, preferred_element_type=F32)
            for q in range(1, Q):
                t = t + lax.dot_general(c_ref[r, col(q)], w[slot, q], NT, preferred_element_type=F32)
            store(r, t.astype(BF16))

    def keys_of(total, slot, read):
        @pl.loop(0, Q)
        def _(q):
            qc = pl.ds(pl.multiple_of(q * wide, 128), wide)
            t = jnp.dot(read(), w[slot, q], preferred_element_type=F32)
            if slot == 0:
                total[:, qc] = t
            else:
                total[:, qc] += t

    def own(slot):
        weights(slot)
        c = cols_of(slot)
        keys_of(acc, slot, lambda: tok[:, c])

        def store(r, v):
            back[r, c] = v

        grad_of(cot, slot, store)

    def pals_back(slot):
        weights(slot)
        need("c", 0, 0)
        need("c", 0, 1)

        def store(r, v):
            backp[slot, r, :] = v

        grad_of(cotp, slot, store)
        ready.add(("back", slot))

    def pals_keys(slot):
        weights(slot)
        need("t", slot, 0)
        keys_of(accp, slot, lambda: tokp[slot])

    def by_rows(f):
        n = toks // 8

        @pl.loop(0, 8)
        def _(i):
            f(pl.ds(pl.multiple_of(i * n, n), n))

    def pals_keys_out():
        def f(r):
            keysp[r, :] = accp[r, :].astype(BF16)

        by_rows(f)
        ready.add("keys")

    def keys_out():
        need("k", 0, 0)

        def f(r):
            keys[r, :] = (acc[r, :] + widen(keysi[r, :])).astype(BF16)

        by_rows(f)

    def send_pair():
        loads["trk"].wait()

        @pl.loop(0, rows // 32)
        def _(i):
            r = pl.ds(pl.multiple_of(i * 32, 32), 32)
            t = trk[r, :]
            mine[0, r, :] = (par[r, :] - 0.01 * t).astype(BF16)
            mine[1, r, :] = t.astype(BF16)

        ready.add("mine")

    def average():
        loads["old"].wait()
        loads["step"].wait()
        for a, i in both:
            need("y", a, i)
            need("f", a, i)
        need("o", 0, 0)
        need("o", 1, 0)
        k = which[0]
        one = [
            jnp.where(k <= 0, 1.0, 0.0), jnp.where(k == 1, 1.0, 0.0), jnp.where(k >= 2, 1.0, 0.0),
        ]

        def partners(a, r):
            t = one[0] * widen(far[0, a, r, :]) + one[1] * widen(far[1, a, r, :])
            return t + one[2] * widen(far[2, a, r, :])

        @pl.loop(0, rows // 32)
        def _(i):
            r = pl.ds(pl.multiple_of(i * 32, 32), 32)
            t = trk[r, :]
            par[r, :] = 0.5 * ((par[r, :] - 0.01 * t) + partners(0, r))
            trk[r, :] = 0.5 * (t + partners(1, r)) - old[r, :]

        ready.add("base")

    def cast(q):
        loads[q].wait()
        w[0, q] = par[:, col(q)].astype(BF16)

    cast(0)
    pl.semaphore_wait(barrier, 6)
    issue("x", 0)
    issue("m", 0)
    loads["cot"].wait()
    issue("p", 0)
    issue("p", 1)
    for name in (1, 2, 3, "trk", "tok", "old", "step"):
        loads[name].start()
    for q in range(1, Q):
        cast(q)
        if q < DEPTH:
            issue("x", q)
            issue("m", q)
    loads["tok"].wait()

    jobs = [
        (0.1, send_pair),
        (0.6, lambda: own(0)),
        (3.5, lambda: pals_back(0)),
        (4.3, lambda: pals_back(1)),
        (4.6, lambda: pals_back(2)),
        (4.9, lambda: sums(3)),
        (5.8, lambda: sums(2)),
        (6.3, lambda: own(1)),
        (6.7, lambda: sums(1)),
        (7.1, lambda: own(2)),
        (7.7, lambda: (pals_keys(0), pals_keys(1), pals_keys(2))),
        (8.1, lambda: (pals_back(3), pals_keys(3), pals_keys_out())),
        (9.2, lambda: own(3)),
        (11.2, average),
        (11.3, lambda: sums(0)),
        (12.7, lambda: add_rows("rx", 0)),
        (13.5, lambda: (add_rows("zf", 0), add_rows("zf", 1))),
        (13.7, lambda: (add_rows("rx", 1), add_rows("zf", 2), add_rows("zf", 3))),
        (14.6, keys_out),
        (14.7, lambda: add_rows("rx", 2)),
    ]
    started = {"x": DEPTH, "p": 2, "m": DEPTH, "y": 0, "f": 0, "o": 0}
    order = [(key, 0, name, i) for key, name, i in program if i >= started[name]]
    order += [(key, 1, "", job) for key, job in jobs]
    for key, kind, name, what in sorted(order, key=lambda e: e[:3]):
        if kind:
            what()
        else:
            issue(name, what)
    add_rows("rx", 3)

    for name, items in links.items():
        for tag, c in items:
            if tag not in seen:
                seen.add(tag)
                c.wait_recv()
        for tag, c in items[-DEPTH:]:
            c.wait_send()


def write_out(keys, back, par, trk, keys_h, back_h, par_h, trk_h, done):
    copies = []
    for src, dst in ((back, back_h), (par, par_h), (trk, trk_h), (keys, keys_h)):
        n = src.shape[0] // 2
        for i in range(2):
            r = pl.ds(i * n, n)
            copies.append(pltpu.make_async_copy(src.at[r], dst.at[0, r], done.at[len(copies)]))
    for c in copies:
        c.start()
    for c in copies:
        c.wait()


def on_device(tokens, cotangent, params, tracker, grad_old, step):
    _, toks, d = tokens.shape
    _, rows, kv = params.shape
    wide = kv // Q
    scale = 1.0 / float(toks * 2 * NZ) ** 0.5
    sem = pltpu.SemaphoreType.DMA
    hbm = pl.BlockSpec(memory_space=pltpu.HBM)
    vmem = pl.BlockSpec(memory_space=pltpu.VMEM)
    results = pl.pallas_call(
        functools.partial(kernel, scale),
        out_shape=(
            pltpu.VMEM((toks, kv), BF16),
            pltpu.VMEM((toks, d), BF16),
            pltpu.VMEM((rows, kv), F32),
            pltpu.VMEM((rows, kv), F32),
        ),
        in_specs=[hbm] * 6,
        out_specs=(vmem,) * 4,
        scratch_shapes=[
            pltpu.VMEM((toks, d), BF16),
            pltpu.VMEM((toks, kv), BF16),
            pltpu.VMEM((rows, kv), F32),
            pltpu.VMEM((4, Q, rows, wide), BF16),
            pltpu.VMEM((3, rows, kv), BF16),
            pltpu.VMEM((4, toks, rows), BF16),
            pltpu.VMEM((toks, kv), BF16),
            pltpu.VMEM((2, rows, kv), BF16),
            pltpu.VMEM((rows, kv), BF16),
            pltpu.VMEM((2, rows, kv), BF16),
            pltpu.VMEM((3, 2, rows, kv), BF16),
            pltpu.VMEM((toks, kv), F32),
            pltpu.VMEM((toks, kv), F32),
            pltpu.VMEM((4, toks, rows), BF16),
            pltpu.VMEM((toks, kv), BF16),
            pltpu.VMEM((toks, kv), BF16),
            pltpu.SMEM((1,), jnp.int32),
            sem((Q + 5,)),
            sem((16,)), sem((16,)), sem((11,)), sem((11,)), sem((9,)), sem((9,)),
            sem((8,)), sem((8,)), sem((8,)), sem((8,)), sem((2,)), sem((2,)),
        ],
        compiler_params=pltpu.CompilerParams(
            collective_id=0, has_side_effects=True, vmem_limit_bytes=50 << 20
        ),
        cost_estimate=pl.CostEstimate(
            flops=6 * toks * d * kv, bytes_accessed=14 << 20, transcendentals=0
        ),
        name="train_step",
    )(tokens, cotangent, params, tracker, grad_old, step)
    return pl.pallas_call(
        write_out,
        out_shape=(
            jax.ShapeDtypeStruct(cotangent.shape, BF16),
            jax.ShapeDtypeStruct(tokens.shape, BF16),
            jax.ShapeDtypeStruct(params.shape, F32),
            jax.ShapeDtypeStruct(params.shape, F32),
        ),
        in_specs=[vmem] * 4,
        out_specs=(hbm,) * 4,
        scratch_shapes=[sem((8,))],
        compiler_params=pltpu.CompilerParams(vmem_limit_bytes=1 << 20),
        name="write_out",
    )(*[pltpu.with_memory_space_constraint(r, pltpu.VMEM) for r in results])


def solution(mesh):
    rows = P("rep", "tp", None)
    return jax.shard_map(
        on_device,
        mesh=mesh,
        in_specs=(rows,) * 5 + (P(),),
        out_specs=(rows,) * 4,
        check_vma=False,
    )
```
